32 devices in a mesh: grp: 2 (over y), tok: 4 (over z), feat: 4 (over x, core).
Axes of the slice: x: 2, y: 2, z: 4, core: 2. Of those that a mesh axis runs over, the one named last changes fastest.
Arguments:
- activations: bfloat16 [8192, 14336], P(('grp', 'tok'), 'feat'), parts along dimension 0, may hold values from -6 to 6
- out_grads: bfloat16 [8192, 4096], P(('grp', 'tok'), 'feat'), parts along dimension 0, may hold values from -6 to 6
- input_side_factors: bfloat16 [8, 32, 14336], P('tok', None, 'feat'), may hold values from -0.046875 to 0.046875
- output_factors: bfloat16 [8, 32, 4096], P('tok', None, 'feat'), may hold values from -0.09375 to 0.09375
- query_order: int32 [8], replicated, may hold values from 0 to 7, each once
Outputs:
- scores: float32 [8192, 8], P(('grp', 'tok', 'feat')), parts along dimension 0
The draws below stay inside these ranges and needn't reach their ends.
There are 2 independent parts, one for each index of `grp`. The reference program is written for one: setup_inputs(seed, part) draws one part's arguments, and reference() takes and returns one part's arrays. A program takes and returns all parts, laid end to end along the dimension named above; an argument that names none is the same for every part. Nothing has to cross between parts.
Inputs may be any that keep to these rules, and one draw needn't show every extreme that they name: `query_order`: each query index appears exactly once.
All inputs are finite; a program needn't handle non-finite values.
Results may differ from the reference program's by a relative error of at most 0.0003.
Values may be sent and summed in bfloat16 or wider, within the bound.
A program may use at most 128 MiB of HBM per device.

```python
import jax
import jax.numpy as jnp

D = 4096
HIDDEN_UNITS = 14336
FACTOR_RANK = 32
QUERY_TOTAL = 8
TOKENS = 4096


def level_of(rng, extent, split, least, largest):
    def one(dim, shards_of):
        draws = jax.random.uniform(jax.random.fold_in(jax.random.fold_in(rng, 6), dim), (shards_of,), jnp.float32, least / len(split), largest / len(split))
        return jnp.repeat(jnp.exp(draws), extent[dim] // shards_of).reshape((-1,) + (1,) * (len(extent) - dim - 1))

    factor_of = one(*split[0])
    for cut in split[1:]:
        factor_of = factor_of * one(*cut)
    return factor_of


def gaussian(key, dims, deviation, most, cuts=(), held_as=jnp.bfloat16):
    loudness = level_of(key, dims, cuts, -0.22, 0.18) if cuts else 1.0
    drawn = jax.random.normal(key, dims, jnp.float32) * deviation * loudness
    return jnp.minimum(jnp.maximum(drawn, -most), most).astype(held_as)


def setup_inputs(seed: int = 0, part: int = 0) -> dict:
    splits = jax.random.split(jax.random.key(seed), 6)
    own_keys = jax.random.split(jax.random.fold_in(splits[5], part), 6)
    return {
        "activations": gaussian(own_keys[0], (TOKENS, HIDDEN_UNITS), 1.0, 6.0, ((0, 4), (1, 4))),
        "out_grads": gaussian(own_keys[1], (TOKENS, D), 1.0, 6.0, ((0, 4), (1, 4))),
        "input_side_factors": gaussian(splits[2], (QUERY_TOTAL, FACTOR_RANK, HIDDEN_UNITS), HIDDEN_UNITS ** -0.5, 0.046875, ((0, 4), (2, 4))),
        "output_factors": gaussian(splits[3], (QUERY_TOTAL, FACTOR_RANK, D), D ** -0.5, 0.09375, ((0, 4), (2, 4))),
        "query_order": jax.random.permutation(splits[4], QUERY_TOTAL).astype(jnp.int32),
    }


def reference(activations, out_grads, input_side_factors, output_factors, query_order):
    right_matrix = input_side_factors.reshape(QUERY_TOTAL * FACTOR_RANK, HIDDEN_UNITS)
    umat = output_factors.reshape(QUERY_TOTAL * FACTOR_RANK, D)
    input_projected = jnp.dot(activations, right_matrix.T, preferred_element_type=jnp.float32)
    output_proj = jnp.dot(out_grads, umat.T, preferred_element_type=jnp.float32)
    prod = (input_projected * output_proj).reshape(TOKENS, QUERY_TOTAL, FACTOR_RANK)
    raw = jnp.sum(prod, axis=2) * (FACTOR_RANK ** -0.5)
    return jnp.take(raw, query_order.astype(jnp.int32), axis=1)
```

```python
import functools

import jax
import jax.numpy as jnp
from jax import lax
from jax.experimental import pallas as pl
from jax.experimental.pallas import tpu as pltpu
from jax.sharding import PartitionSpec as P

MESH = pl.DeviceIdType.MESH
NT = (((1,), (1,)), ((), ()))
PIECES = 3


def segments(left_half, right_half):
    width = (left_half + right_half) // PIECES
    result = []
    for j in range(PIECES):
        lo, hi = j * width, (j + 1) * width
        segs = []
        if lo < left_half:
            segs.append((False, lo, 0, min(hi, left_half) - lo))
        if hi > left_half:
            start = max(lo, left_half)
            segs.append((True, start - left_half, start - lo, hi - start))
        result.append(segs)
    return width, result


def fused(n, rank, a_hbm, g_hbm, v_hbm, u_hbm, order_ref, out_ref,
          a, g, w, part, core_in, pair, pair_in,
          load_a, load_w, z_send, z_recv, y_send, y_recv,
          c_send, c_recv, x_send, x_recv):
    y, z, f = lax.axis_index("grp"), lax.axis_index("tok"), lax.axis_index("feat")
    c, x = lax.rem(f, 2), lax.div(f, 2)
    left_half, right_half = a.shape[1] // 2, g.shape[1] // 2
    width, segs = segments(left_half, right_half)
    rows = w.shape[3]
    chunk = out_ref.shape[1]
    core_mate, x_mate = 2 * x + (1 - c), 2 * (1 - x) + c

    def own_loads(which, h, j):
        made = []
        for i, (is_right, off, at, wide) in enumerate(segs[j]):
            src = u_hbm if is_right else v_hbm
            half = right_half if is_right else left_half
            made.append(pltpu.make_async_copy(
                src.at[:, pl.ds(pl.multiple_of(h * half + off, 128), wide)],
                w.at[z, h, j, :, pl.ds(at, wide)],
                load_w.at[which, j, i]))
        return made

    for which, h in ((0, y), (1, 1 - y)):
        for j in range(PIECES):
            for copy in own_loads(which, h, j):
                copy.start()
    copy_a = pltpu.make_async_copy(a_hbm, a, load_a.at[0])
    copy_g = pltpu.make_async_copy(g_hbm, g, load_a.at[1])
    copy_a.start()
    copy_g.start()

    barrier = pltpu.get_barrier_semaphore()
    pl.semaphore_signal(barrier, inc=1, device_id={"grp": 1 - y}, device_id_type=MESH)
    pl.semaphore_signal(barrier, inc=1, device_id={"feat": core_mate}, device_id_type=MESH)
    pl.semaphore_signal(barrier, inc=1, device_id={"feat": x_mate}, device_id_type=MESH)

    @pl.when(z > 0)
    def _():
        pl.semaphore_signal(barrier, inc=1, device_id={"tok": z - 1}, device_id_type=MESH)

    @pl.when(z < n - 1)
    def _():
        pl.semaphore_signal(barrier, inc=1, device_id={"tok": z + 1}, device_id_type=MESH)

    peers = 3 + jnp.where(z > 0, 1, 0) + jnp.where(z < n - 1, 1, 0)
    pl.semaphore_wait(barrier, peers)

    def source(way, d):
        return z - d if way == 0 else z + d

    def arrives(way, d):
        return z >= d if way == 0 else z < n - d

    def has_next(way):
        return z < n - 1 if way == 0 else z > 0

    def z_copy(way, d, j, s):
        return pltpu.make_async_remote_copy(
            src_ref=w.at[s, y, j], dst_ref=w.at[s, y, j],
            send_sem=z_send.at[way, d - 1, j], recv_sem=z_recv.at[way, d - 1, j],
            device_id={"tok": z + 1 if way == 0 else z - 1}, device_id_type=MESH)

    def y_copy(way, d, j, h):
        s = source(way, d)
        return pltpu.make_async_remote_copy(
            src_ref=w.at[s, h, j], dst_ref=w.at[s, h, j],
            send_sem=y_send.at[way, d - 1, j], recv_sem=y_recv.at[way, d - 1, j],
            device_id={"grp": 1 - y}, device_id_type=MESH)

    def core_copy(b):
        return pltpu.make_async_remote_copy(
            src_ref=part.at[b, 1 - c], dst_ref=core_in.at[b],
            send_sem=c_send.at[b], recv_sem=c_recv.at[b],
            device_id={"feat": core_mate}, device_id_type=MESH)

    def x_copy(b):
        return pltpu.make_async_remote_copy(
            src_ref=pair.at[b], dst_ref=pair_in.at[b],
            send_sem=x_send.at[b], recv_sem=x_recv.at[b],
            device_id={"feat": x_mate}, device_id_type=MESH)

    def add_piece(b, s, h, j, fresh):
        def some_rows(m, carry):
            at_rows = pl.ds(pl.multiple_of(m * chunk, chunk), chunk)
            for is_right, off, at, wide in segs[j]:
                side = g if is_right else a
                half = right_half if is_right else left_half
                columns = pl.ds(pl.multiple_of(h * half + off, 128), wide)
                product = lax.dot_general(
                    side[at_rows, columns], w[s, h, j, :, pl.ds(at, wide)], NT,
                    preferred_element_type=jnp.float32)
                to = (b, lax.rem(m, 2), lax.div(m, 2), slice(None),
                      pl.ds(rows if is_right else 0, rows))
                if fresh and off == 0:
                    part[to] = product
                else:
                    part[to] += product
            return carry

        lax.fori_loop(0, a.shape[0] // chunk, some_rows, 0)

    def across_x(b):
        core_copy(b).wait_recv()
        pair[b] = part[b, c, 1 - x] + core_in[b, 1 - x]
        x_copy(b).start()

    def finish(b, s):
        x_copy(b).wait_recv()
        total = part[b, c, x] + core_in[b, x] + pair_in[b]
        product = total[:, :rows] * total[:, rows:]
        query = s * (rows // rank) + lax.div(
            lax.broadcasted_iota(jnp.int32, (out_ref.shape[0], rows), 1), rank)
        pick = jnp.where(query == order_ref[...], 1.0, 0.0).astype(jnp.float32)
        out_ref[...] += lax.dot_general(
            pick, product, NT, precision=lax.Precision.HIGHEST,
            preferred_element_type=jnp.float32) * (rank ** -0.5)

    def block(way, d):
        return 1 + 2 * (d - 1) + way

    out_ref[...] = jnp.zeros_like(out_ref)
    for j in range(PIECES):
        for copy in own_loads(0, y, j):
            copy.wait()
        for way in (0, 1):
            @pl.when(has_next(way))
            def _():
                z_copy(way, 1, j, z).start()

    def each_way(d, action):
        for way in (0, 1):
            @pl.when(arrives(way, d))
            def _():
                action(way)

    slots = [(d, j) for d in range(1, n) for j in range(PIECES)]

    def other_half(d, j):
        def action(way):
            y_copy(way, d, j, 1 - y).wait_recv()
            add_piece(block(way, d), source(way, d), 1 - y, j, False)
            if j == PIECES - 1:
                core_copy(block(way, d)).start()
        each_way(d, action)

    for k, (d, j) in enumerate(slots):
        def pass_on(way):
            s = source(way, d)
            z_copy(way, d, j, s).wait_recv()
            y_copy(way, d, j, y).start()
            if d < n - 1:
                @pl.when(has_next(way))
                def _():
                    z_copy(way, d + 1, j, s).start()
        each_way(d, pass_on)
        if d == 1:
            if j == 0:
                for jj in range(PIECES):
                    for copy in own_loads(1, 1 - y, jj):
                        copy.wait()
                copy_a.wait()
                copy_g.wait()
            add_piece(0, z, 0, j, True)
            add_piece(0, z, 1, j, False)
            if j == PIECES - 1:
                core_copy(0).start()
        each_way(d, lambda way: add_piece(block(way, d), source(way, d), y, j, True))
        if k >= 1:
            other_half(*slots[k - 1])
        if j == 1:
            if d == 2:
                across_x(0)
            if d >= 2:
                each_way(d - 1, lambda way: across_x(block(way, d - 1)))
        if j == PIECES - 1:
            if d == 2:
                finish(0, z)
            if d >= 3:
                each_way(d - 2, lambda way: finish(block(way, d - 2), source(way, d - 2)))
    other_half(*slots[-1])
    each_way(n - 1, lambda way: across_x(block(way, n - 1)))
    for d in range(max(n - 2, 1), n):
        each_way(d, lambda way: finish(block(way, d), source(way, d)))

    for way in (0, 1):
        for d in range(1, n):
            sends = (arrives(way, d - 1) if d > 1 else z >= 0) & has_next(way)

            @pl.when(sends)
            def _():
                for j in range(PIECES):
                    z_copy(way, d, j, source(way, d - 1)).wait_send()

            @pl.when(arrives(way, d))
            def _():
                for j in range(PIECES):
                    y_copy(way, d, j, y).wait_send()
                core_copy(block(way, d)).wait_send()
                x_copy(block(way, d)).wait_send()
    core_copy(0).wait_send()
    x_copy(0).wait_send()


def fused_shards(n, activations, out_grads, input_side_factors, output_factors, query_order):
    per_block, rank, left = input_side_factors.shape
    right = output_factors.shape[2]
    rows = per_block * rank
    tokens = activations.shape[0]
    chunk = tokens // 4
    total = query_order.shape[0]
    width, segs = segments(left // 2, right // 2)
    most = max(len(s) for s in segs)
    blocks = 2 * n - 1
    dma = pltpu.SemaphoreType.DMA
    f32 = jnp.float32
    return pl.pallas_call(
        functools.partial(fused, n, rank),
        out_shape=jax.ShapeDtypeStruct((total, chunk), f32),
        in_specs=[pl.BlockSpec(memory_space=pl.ANY)] * 4 + [pl.BlockSpec(memory_space=pltpu.VMEM)],
        out_specs=pl.BlockSpec(memory_space=pltpu.VMEM),
        scratch_shapes=[
            pltpu.VMEM((tokens, left), activations.dtype),
            pltpu.VMEM((tokens, right), out_grads.dtype),
            pltpu.VMEM((n, 2, PIECES, rows, width), input_side_factors.dtype),
            pltpu.VMEM((blocks, 2, 2, chunk, 2 * rows), f32),
            pltpu.VMEM((blocks, 2, chunk, 2 * rows), f32),
            pltpu.VMEM((blocks, chunk, 2 * rows), f32),
            pltpu.VMEM((blocks, chunk, 2 * rows), f32),
            dma((2,)),
            dma((2, PIECES, most)),
            dma((2, n - 1, PIECES)),
            dma((2, n - 1, PIECES)),
            dma((2, n - 1, PIECES)),
            dma((2, n - 1, PIECES)),
            dma((blocks,)),
            dma((blocks,)),
            dma((blocks,)),
            dma((blocks,)),
        ],
        compiler_params=pltpu.CompilerParams(
            collective_id=0, has_side_effects=True, vmem_limit_bytes=60 * 2**20),
        cost_estimate=pl.CostEstimate(
            flops=2 * tokens * n * rows * (left + right),
            bytes_accessed=2 * (tokens + rows) * (left + right), transcendentals=0),
    )(
        activations, out_grads,
        input_side_factors.reshape(rows, left), output_factors.reshape(rows, right),
        query_order.reshape(total, 1),
    ).T


def plain_shards(activations, out_grads, input_side_factors, output_factors, query_order):
    rank = input_side_factors.shape[1]
    all_v = lax.all_gather(input_side_factors, "tok", axis=0, tiled=True)
    all_u = lax.all_gather(output_factors, "tok", axis=0, tiled=True)
    sides = []
    for tokens, factors in ((activations, all_v), (out_grads, all_u)):
        matrix = factors.reshape(-1, factors.shape[2])
        partial = lax.dot_general(tokens, matrix, NT, preferred_element_type=jnp.float32)
        sides.append(lax.psum_scatter(partial, "feat", scatter_dimension=0, tiled=True))
    product = (sides[0] * sides[1]).reshape(sides[0].shape[0], -1, rank)
    return jnp.take(jnp.sum(product, axis=2) * rank ** (-0.5), query_order, axis=1)


def solution(mesh):
    n = mesh.shape["tok"]
    small = n <= 4 and mesh.shape["grp"] == 2 and mesh.shape["feat"] == 4
    return jax.shard_map(
        functools.partial(fused_shards, n) if small else plain_shards,
        mesh=mesh,
        in_specs=(
            P(("grp", "tok"), "feat"),
            P(("grp", "tok"), "feat"),
            P("tok", None, "feat"),
            P("tok", None, "feat"),
            P(),
        ),
        out_specs=P(("grp", "tok", "feat"), None),
        check_vma=False,
    )
```

```python
import functools

import jax
import jax.numpy as jnp
from jax import lax
from jax.experimental import pallas as pl
from jax.experimental.pallas import tpu as pltpu
from jax.sharding import PartitionSpec as P

MESH = pl.DeviceIdType.MESH
NT = (((1,), (1,)), ((), ()))
PIECES = 2


def segments(left_half, right_half):
    width = (left_half + right_half) // PIECES
    result = []
    for j in range(PIECES):
        lo, hi = j * width, (j + 1) * width
        segs = []
        if lo < left_half:
            segs.append((False, lo, 0, min(hi, left_half) - lo))
        if hi > left_half:
            start = max(lo, left_half)
            segs.append((True, start - left_half, start - lo, hi - start))
        result.append(segs)
    return width, result


def fused(n, rank, a_hbm, g_hbm, v_hbm, u_hbm, order_ref, out_ref,
          a, g, w, part, core_in, pair, pair_in,
          load_a, load_w, z_send, z_recv, y_send, y_recv,
          c_send, c_recv, x_send, x_recv):
    y, z, f = lax.axis_index("grp"), lax.axis_index("tok"), lax.axis_index("feat")
    c, x = lax.rem(f, 2), lax.div(f, 2)
    left_half, right_half = a.shape[1] // 2, g.shape[1] // 2
    width, segs = segments(left_half, right_half)
    rows = w.shape[3]
    chunk = out_ref.shape[1]
    core_mate, x_mate = 2 * x + (1 - c), 2 * (1 - x) + c

    def own_loads(which, h, j):
        made = []
        for i, (is_right, off, at, wide) in enumerate(segs[j]):
            src = u_hbm if is_right else v_hbm
            half = right_half if is_right else left_half
            made.append(pltpu.make_async_copy(
                src.at[:, pl.ds(pl.multiple_of(h * half + off, 128), wide)],
                w.at[z, h, j, :, pl.ds(at, wide)],
                load_w.at[which, j, i]))
        return made

    for which, h in ((0, y), (1, 1 - y)):
        for j in range(PIECES):
            for copy in own_loads(which, h, j):
                copy.start()
    copy_a = pltpu.make_async_copy(a_hbm, a, load_a.at[0])
    copy_g = pltpu.make_async_copy(g_hbm, g, load_a.at[1])
    copy_a.start()
    copy_g.start()

    barrier = pltpu.get_barrier_semaphore()
    pl.semaphore_signal(barrier, inc=1, device_id={"grp": 1 - y}, device_id_type=MESH)
    pl.semaphore_signal(barrier, inc=1, device_id={"feat": core_mate}, device_id_type=MESH)
    pl.semaphore_signal(barrier, inc=1, device_id={"feat": x_mate}, device_id_type=MESH)

    @pl.when(z > 0)
    def _():
        pl.semaphore_signal(barrier, inc=1, device_id={"tok": z - 1}, device_id_type=MESH)

    @pl.when(z < n - 1)
    def _():
        pl.semaphore_signal(barrier, inc=1, device_id={"tok": z + 1}, device_id_type=MESH)

    peers = 3 + jnp.where(z > 0, 1, 0) + jnp.where(z < n - 1, 1, 0)
    pl.semaphore_wait(barrier, peers)

    def source(way, d):
        return z - d if way == 0 else z + d

    def arrives(way, d):
        return z >= d if way == 0 else z < n - d

    def has_next(way):
        return z < n - 1 if way == 0 else z > 0

    def z_copy(way, d, j, s):
        return pltpu.make_async_remote_copy(
            src_ref=w.at[s, y, j], dst_ref=w.at[s, y, j],
            send_sem=z_send.at[way, d - 1, j], recv_sem=z_recv.at[way, d - 1, j],
            device_id={"tok": z + 1 if way == 0 else z - 1}, device_id_type=MESH)

    def y_copy(way, d, j, h):
        s = source(way, d)
        return pltpu.make_async_remote_copy(
            src_ref=w.at[s, h, j], dst_ref=w.at[s, h, j],
            send_sem=y_send.at[way, d - 1, j], recv_sem=y_recv.at[way, d - 1, j],
            device_id={"grp": 1 - y}, device_id_type=MESH)

    def core_copy(b):
        return pltpu.make_async_remote_copy(
            src_ref=part.at[b, 1 - c], dst_ref=core_in.at[b],
            send_sem=c_send.at[b], recv_sem=c_recv.at[b],
            device_id={"feat": core_mate}, device_id_type=MESH)

    def x_copy(b):
        return pltpu.make_async_remote_copy(
            src_ref=pair.at[b], dst_ref=pair_in.at[b],
            send_sem=x_send.at[b], recv_sem=x_recv.at[b],
            device_id={"feat": x_mate}, device_id_type=MESH)

    def add_piece(b, s, h, j, fresh):
        for is_right, off, at, wide in segs[j]:
            side = g if is_right else a
            half = right_half if is_right else left_half
            columns = pl.ds(pl.multiple_of(h * half + off, 128), wide)
            product = lax.dot_general(
                side[:, columns], w[s, h, j, :, pl.ds(at, wide)], NT,
                preferred_element_type=jnp.float32)
            for m in range(4):
                to = (b, m % 2, m // 2, slice(None), pl.ds(rows if is_right else 0, rows))
                some = product[m * chunk:(m + 1) * chunk]
                if fresh and off == 0:
                    part[to] = some
                else:
                    part[to] += some

    def across_x(b):
        core_copy(b).wait_recv()
        pair[b] = part[b, c, 1 - x] + core_in[b, 1 - x]
        x_copy(b).start()

    def finish(b, s):
        x_copy(b).wait_recv()
        total = part[b, c, x] + core_in[b, x] + pair_in[b]
        product = total[:, :rows] * total[:, rows:]
        query = s * (rows // rank) + lax.div(
            lax.broadcasted_iota(jnp.int32, (out_ref.shape[0], rows), 1), rank)
        column = lax.broadcasted_iota(jnp.int32, query.shape, 0)
        wanted = jnp.zeros_like(query)
        for k in range(out_ref.shape[0]):
            wanted = jnp.where(column == k, order_ref[k], wanted)
        pick = jnp.where(query == wanted, 1.0, 0.0).astype(jnp.float32)
        out_ref[...] += lax.dot_general(
            pick, product, NT, precision=lax.Precision.HIGHEST,
            preferred_element_type=jnp.float32) * (rank ** -0.5)

    def block(way, d):
        return 1 + 2 * (d - 1) + way

    out_ref[...] = jnp.zeros_like(out_ref)
    for j in range(PIECES):
        for copy in own_loads(0, y, j):
            copy.wait()
        for way in (0, 1):
            @pl.when(has_next(way))
            def _():
                z_copy(way, 1, j, z).start()

    def each_way(d, action):
        for way in (0, 1):
            @pl.when(arrives(way, d))
            def _():
                action(way)

    slots = [(d, j) for d in range(1, n) for j in range(PIECES)]

    def other_half(d, j):
        def action(way):
            y_copy(way, d, j, 1 - y).wait_recv()
            add_piece(block(way, d), source(way, d), 1 - y, j, False)
            if j == PIECES - 1:
                core_copy(block(way, d)).start()
        each_way(d, action)

    for k, (d, j) in enumerate(slots):
        def pass_on(way):
            s = source(way, d)
            z_copy(way, d, j, s).wait_recv()
            y_copy(way, d, j, y).start()
            if d < n - 1:
                @pl.when(has_next(way))
                def _():
                    z_copy(way, d + 1, j, s).start()
        each_way(d, pass_on)
        if d == 1:
            if j == 0:
                for jj in range(PIECES):
                    for copy in own_loads(1, 1 - y, jj):
                        copy.wait()
                copy_a.wait()
                copy_g.wait()
            add_piece(0, z, 0, j, True)
            add_piece(0, z, 1, j, False)
            if j == PIECES - 1:
                core_copy(0).start()
        each_way(d, lambda way: add_piece(block(way, d), source(way, d), y, j, True))
        if k >= 1:
            other_half(*slots[k - 1])
        if j == min(1, PIECES - 1):
            if d == 2:
                across_x(0)
            if d >= 2:
                each_way(d - 1, lambda way: across_x(block(way, d - 1)))
        if j == PIECES - 1:
            if d == 2:
                finish(0, z)
            if d >= 3:
                each_way(d - 2, lambda way: finish(block(way, d - 2), source(way, d - 2)))
    other_half(*slots[-1])
    each_way(n - 1, lambda way: across_x(block(way, n - 1)))
    for d in range(max(n - 2, 1), n):
        each_way(d, lambda way: finish(block(way, d), source(way, d)))

    for way in (0, 1):
        for d in range(1, n):
            sends = (arrives(way, d - 1) if d > 1 else z >= 0) & has_next(way)

            @pl.when(sends)
            def _():
                for j in range(PIECES):
                    z_copy(way, d, j, source(way, d - 1)).wait_send()

            @pl.when(arrives(way, d))
            def _():
                for j in range(PIECES):
                    y_copy(way, d, j, y).wait_send()
                core_copy(block(way, d)).wait_send()
                x_copy(block(way, d)).wait_send()
    core_copy(0).wait_send()
    x_copy(0).wait_send()


def fused_shards(n, activations, out_grads, input_side_factors, output_factors, query_order):
    per_block, rank, left = input_side_factors.shape
    right = output_factors.shape[2]
    rows = per_block * rank
    tokens = activations.shape[0]
    chunk = tokens // 4
    total = query_order.shape[0]
    width, segs = segments(left // 2, right // 2)
    most = max(len(s) for s in segs)
    blocks = 2 * n - 1
    dma = pltpu.SemaphoreType.DMA
    f32 = jnp.float32
    return pl.pallas_call(
        functools.partial(fused, n, rank),
        out_shape=jax.ShapeDtypeStruct((total, chunk), f32),
        in_specs=[pl.BlockSpec(memory_space=pl.ANY)] * 4 + [pl.BlockSpec(memory_space=pltpu.SMEM)],
        out_specs=pl.BlockSpec(memory_space=pltpu.VMEM),
        scratch_shapes=[
            pltpu.VMEM((tokens, left), activations.dtype),
            pltpu.VMEM((tokens, right), out_grads.dtype),
            pltpu.VMEM((n, 2, PIECES, rows, width), input_side_factors.dtype),
            pltpu.VMEM((blocks, 2, 2, chunk, 2 * rows), f32),
            pltpu.VMEM((blocks, 2, chunk, 2 * rows), f32),
            pltpu.VMEM((blocks, chunk, 2 * rows), f32),
            pltpu.VMEM((blocks, chunk, 2 * rows), f32),
            dma((2,)),
            dma((2, PIECES, most)),
            dma((2, n - 1, PIECES)),
            dma((2, n - 1, PIECES)),
            dma((2, n - 1, PIECES)),
            dma((2, n - 1, PIECES)),
            dma((blocks,)),
            dma((blocks,)),
            dma((blocks,)),
            dma((blocks,)),
        ],
        compiler_params=pltpu.CompilerParams(
            collective_id=0, has_side_effects=True, vmem_limit_bytes=60 * 2**20),
        cost_estimate=pl.CostEstimate(
            flops=2 * tokens * n * rows * (left + right),
            bytes_accessed=2 * (tokens + rows) * (left + right), transcendentals=0),
    )(
        activations, out_grads,
        input_side_factors.reshape(rows, left), output_factors.reshape(rows, right),
        query_order,
    ).T


def plain_shards(activations, out_grads, input_side_factors, output_factors, query_order):
    rank = input_side_factors.shape[1]
    all_v = lax.all_gather(input_side_factors, "tok", axis=0, tiled=True)
    all_u = lax.all_gather(output_factors, "tok", axis=0, tiled=True)
    sides = []
    for tokens, factors in ((activations, all_v), (out_grads, all_u)):
        matrix = factors.reshape(-1, factors.shape[2])
        partial = lax.dot_general(tokens, matrix, NT, preferred_element_type=jnp.float32)
        sides.append(lax.psum_scatter(partial, "feat", scatter_dimension=0, tiled=True))
    product = (sides[0] * sides[1]).reshape(sides[0].shape[0], -1, rank)
    return jnp.take(jnp.sum(product, axis=2) * rank ** (-0.5), query_order, axis=1)


def solution(mesh):
    n = mesh.shape["tok"]
    small = n <= 4 and mesh.shape["grp"] == 2 and mesh.shape["feat"] == 4
    return jax.shard_map(
        functools.partial(fused_shards, n) if small else plain_shards,
        mesh=mesh,
        in_specs=(
            P(("grp", "tok"), "feat"),
            P(("grp", "tok"), "feat"),
            P("tok", None, "feat"),
            P("tok", None, "feat"),
            P(),
        ),
        out_specs=P(("grp", "tok", "feat"), None),
        check_vma=False,
    )
```

```python
import functools

import jax
import jax.numpy as jnp
from jax import lax
from jax.experimental import pallas as pl
from jax.experimental.pallas import tpu as pltpu
from jax.sharding import PartitionSpec as P

MESH = pl.DeviceIdType.MESH
NT = (((1,), (1,)), ((), ()))
PIECES = 3


def segments(left_half, right_half):
    width = (left_half + right_half) // PIECES
    result = []
    for j in range(PIECES):
        lo, hi = j * width, (j + 1) * width
        segs = []
        if lo < left_half:
            segs.append((False, lo, 0, min(hi, left_half) - lo))
        if hi > left_half:
            start = max(lo, left_half)
            segs.append((True, start - left_half, start - lo, hi - start))
        result.append(segs)
    return width, result


def fused(n, rank, a_hbm, g_hbm, v_hbm, u_hbm, order_ref, out_ref,
          a, g, w, part, core_in, pair, pair_in,
          load_a, load_w, z_send, z_recv, y_send, y_recv,
          c_send, c_recv, x_send, x_recv, e_send, e_recv):
    y, z, f = lax.axis_index("grp"), lax.axis_index("tok"), lax.axis_index("feat")
    c, x = lax.rem(f, 2), lax.div(f, 2)
    left_half, right_half = a.shape[1] // 2, g.shape[1] // 2
    width, segs = segments(left_half, right_half)
    rows, last = w.shape[3], PIECES - 1
    chunk = out_ref.shape[1]
    core_mate, x_mate = 2 * x + (1 - c), 2 * (1 - x) + c

    def own_loads(which, h, j):
        made = []
        for i, (is_right, off, at, wide) in enumerate(segs[j]):
            src = u_hbm if is_right else v_hbm
            half = right_half if is_right else left_half
            made.append(pltpu.make_async_copy(
                src.at[:, pl.ds(pl.multiple_of(h * half + off, 128), wide)],
                w.at[z, h, j, :, pl.ds(at, wide)],
                load_w.at[which, j, i]))
        return made

    for which, h in ((0, y), (1, 1 - y)):
        for j in range(PIECES):
            for copy in own_loads(which, h, j):
                copy.start()
    copy_a = pltpu.make_async_copy(a_hbm, a, load_a.at[0])
    copy_g = pltpu.make_async_copy(g_hbm, g, load_a.at[1])
    copy_a.start()
    copy_g.start()

    barrier = pltpu.get_barrier_semaphore()
    pl.semaphore_signal(barrier, inc=1, device_id={"grp": 1 - y}, device_id_type=MESH)
    pl.semaphore_signal(barrier, inc=1, device_id={"feat": core_mate}, device_id_type=MESH)
    pl.semaphore_signal(barrier, inc=1, device_id={"feat": x_mate}, device_id_type=MESH)

    @pl.when(z > 0)
    def _():
        pl.semaphore_signal(barrier, inc=1, device_id={"tok": z - 1}, device_id_type=MESH)

    @pl.when(z < n - 1)
    def _():
        pl.semaphore_signal(barrier, inc=1, device_id={"tok": z + 1}, device_id_type=MESH)

    peers = 3 + jnp.where(z > 0, 1, 0) + jnp.where(z < n - 1, 1, 0)
    pl.semaphore_wait(barrier, peers)

    def source(way, d):
        return z - d if way == 0 else z + d

    def arrives(way, d):
        return z >= d if way == 0 else z < n - d

    def has_next(way):
        return z < n - 1 if way == 0 else z > 0

    def z_copy(way, d, j, s):
        return pltpu.make_async_remote_copy(
            src_ref=w.at[s, y, j], dst_ref=w.at[s, y, j],
            send_sem=z_send.at[way, d - 1, j], recv_sem=z_recv.at[way, d - 1, j],
            device_id={"tok": z + 1 if way == 0 else z - 1}, device_id_type=MESH)

    def from_end(way, d):
        return z == d if way == 0 else z == n - 1 - d

    def extra_copy(way, d, s):
        return pltpu.make_async_remote_copy(
            src_ref=w.at[s, 1 - y, last], dst_ref=w.at[s, 1 - y, last],
            send_sem=e_send.at[way, d - 1], recv_sem=e_recv.at[way, d - 1],
            device_id={"tok": z + 1 if way == 0 else z - 1}, device_id_type=MESH)

    def unless_extra(way, d, j, action):
        if j == last:
            pl.when(jnp.logical_not(from_end(way, d)))(action)
        else:
            action()

    def y_copy(way, d, j, h):
        s = source(way, d)
        return pltpu.make_async_remote_copy(
            src_ref=w.at[s, h, j], dst_ref=w.at[s, h, j],
            send_sem=y_send.at[way, d - 1, j], recv_sem=y_recv.at[way, d - 1, j],
            device_id={"grp": 1 - y}, device_id_type=MESH)

    def core_copy(b):
        return pltpu.make_async_remote_copy(
            src_ref=part.at[b, 1 - c], dst_ref=core_in.at[b],
            send_sem=c_send.at[b], recv_sem=c_recv.at[b],
            device_id={"feat": core_mate}, device_id_type=MESH)

    def x_copy(b):
        return pltpu.make_async_remote_copy(
            src_ref=pair.at[b], dst_ref=pair_in.at[b],
            send_sem=x_send.at[b], recv_sem=x_recv.at[b],
            device_id={"feat": x_mate}, device_id_type=MESH)

    def add_piece(b, s, h, j, fresh):
        for is_right, off, at, wide in segs[j]:
            side = g if is_right else a
            half = right_half if is_right else left_half
            columns = pl.ds(pl.multiple_of(h * half + off, 128), wide)
            product = lax.dot_general(
                side[:, columns], w[s, h, j, :, pl.ds(at, wide)], NT,
                preferred_element_type=jnp.float32)
            for m in range(4):
                to = (b, m % 2, m // 2, slice(None), pl.ds(rows if is_right else 0, rows))
                some = product[m * chunk:(m + 1) * chunk]
                if fresh and off == 0:
                    part[to] = some
                else:
                    part[to] += some

    def across_x(b):
        core_copy(b).wait_recv()
        pair[b] = part[b, c, 1 - x] + core_in[b, 1 - x]
        x_copy(b).start()

    def finish(b, s):
        x_copy(b).wait_recv()
        total = part[b, c, x] + core_in[b, x] + pair_in[b]
        product = total[:, :rows] * total[:, rows:]
        query = s * (rows // rank) + lax.div(
            lax.broadcasted_iota(jnp.int32, (out_ref.shape[0], rows), 1), rank)
        column = lax.broadcasted_iota(jnp.int32, query.shape, 0)
        wanted = jnp.zeros_like(query)
        for k in range(out_ref.shape[0]):
            wanted = jnp.where(column == k, order_ref[k], wanted)
        pick = jnp.where(query == wanted, 1.0, 0.0).astype(jnp.float32)
        out_ref[...] += lax.dot_general(
            pick, product, NT, precision=lax.Precision.HIGHEST,
            preferred_element_type=jnp.float32) * (rank ** -0.5)

    def block(way, d):
        return 1 + 2 * (d - 1) + way

    out_ref[...] = jnp.zeros_like(out_ref)
    for j in range(PIECES):
        for copy in own_loads(0, y, j):
            copy.wait()
        for way in (0, 1):
            @pl.when(has_next(way))
            def _():
                z_copy(way, 1, j, z).start()
    for j in range(PIECES):
        for copy in own_loads(1, 1 - y, j):
            copy.wait()
    for way in (0, 1):
        @pl.when(from_end(way, 0))
        def _():
            extra_copy(way, 1, z).start()

    def each_way(d, action):
        for way in (0, 1):
            @pl.when(arrives(way, d))
            def _():
                action(way)

    slots = [(d, j) for d in range(1, n) for j in range(PIECES)]

    def other_half(d, j):
        def action(way):
            unless_extra(way, d, j, lambda: y_copy(way, d, j, 1 - y).wait_recv())
            add_piece(block(way, d), source(way, d), 1 - y, j, False)
            if j == PIECES - 1:
                core_copy(block(way, d)).start()
        each_way(d, action)

    for k, (d, j) in enumerate(slots):
        def pass_on(way):
            s = source(way, d)
            z_copy(way, d, j, s).wait_recv()
            unless_extra(way, d, j, lambda: y_copy(way, d, j, y).start())
            if d < n - 1:
                @pl.when(has_next(way))
                def _():
                    z_copy(way, d + 1, j, s).start()
        each_way(d, pass_on)
        if d == 1:
            if j == 0:
                copy_a.wait()
                copy_g.wait()
            add_piece(0, z, 0, j, True)
            add_piece(0, z, 1, j, False)
            if j == PIECES - 1:
                core_copy(0).start()
        each_way(d, lambda way: add_piece(block(way, d), source(way, d), y, j, True))
        if k >= 1:
            other_half(*slots[k - 1])
        if j == last:
            for way in (0, 1):
                @pl.when(from_end(way, d))
                def _():
                    extra_copy(way, d, source(way, d)).wait_recv()
                    if d < n - 1:
                        extra_copy(way, d + 1, source(way, d)).start()
        if j == min(1, PIECES - 1):
            if d == 2:
                across_x(0)
            if d >= 2:
                each_way(d - 1, lambda way: across_x(block(way, d - 1)))
        if j == PIECES - 1:
            if d == 2:
                finish(0, z)
            if d >= 3:
                each_way(d - 2, lambda way: finish(block(way, d - 2), source(way, d - 2)))
    other_half(*slots[-1])
    each_way(n - 1, lambda way: across_x(block(way, n - 1)))
    for d in range(max(n - 2, 1), n):
        each_way(d, lambda way: finish(block(way, d), source(way, d)))

    for way in (0, 1):
        for d in range(1, n):
            @pl.when(from_end(way, d - 1))
            def _():
                extra_copy(way, d, source(way, d - 1)).wait_send()

            sends = (arrives(way, d - 1) if d > 1 else z >= 0) & has_next(way)

            @pl.when(sends)
            def _():
                for j in range(PIECES):
                    z_copy(way, d, j, source(way, d - 1)).wait_send()

            @pl.when(arrives(way, d))
            def _():
                for j in range(PIECES):
                    unless_extra(way, d, j, lambda: y_copy(way, d, j, y).wait_send())
                core_copy(block(way, d)).wait_send()
                x_copy(block(way, d)).wait_send()
    core_copy(0).wait_send()
    x_copy(0).wait_send()


def fused_shards(n, activations, out_grads, input_side_factors, output_factors, query_order):
    per_block, rank, left = input_side_factors.shape
    right = output_factors.shape[2]
    rows = per_block * rank
    tokens = activations.shape[0]
    chunk = tokens // 4
    total = query_order.shape[0]
    width, segs = segments(left // 2, right // 2)
    most = max(len(s) for s in segs)
    blocks = 2 * n - 1
    dma = pltpu.SemaphoreType.DMA
    f32 = jnp.float32
    return pl.pallas_call(
        functools.partial(fused, n, rank),
        out_shape=jax.ShapeDtypeStruct((total, chunk), f32),
        in_specs=[pl.BlockSpec(memory_space=pl.ANY)] * 4 + [pl.BlockSpec(memory_space=pltpu.SMEM)],
        out_specs=pl.BlockSpec(memory_space=pltpu.VMEM),
        scratch_shapes=[
            pltpu.VMEM((tokens, left), activations.dtype),
            pltpu.VMEM((tokens, right), out_grads.dtype),
            pltpu.VMEM((n, 2, PIECES, rows, width), input_side_factors.dtype),
            pltpu.VMEM((blocks, 2, 2, chunk, 2 * rows), f32),
            pltpu.VMEM((blocks, 2, chunk, 2 * rows), f32),
            pltpu.VMEM((blocks, chunk, 2 * rows), f32),
            pltpu.VMEM((blocks, chunk, 2 * rows), f32),
            dma((2,)),
            dma((2, PIECES, most)),
            dma((2, n - 1, PIECES)),
            dma((2, n - 1, PIECES)),
            dma((2, n - 1, PIECES)),
            dma((2, n - 1, PIECES)),
            dma((blocks,)),
            dma((blocks,)),
            dma((blocks,)),
            dma((blocks,)),
            dma((2, n - 1)),
            dma((2, n - 1)),
        ],
        compiler_params=pltpu.CompilerParams(
            collective_id=0, has_side_effects=True, vmem_limit_bytes=60 * 2**20),
        cost_estimate=pl.CostEstimate(
            flops=2 * tokens * n * rows * (left + right),
            bytes_accessed=2 * (tokens + rows) * (left + right), transcendentals=0),
    )(
        activations, out_grads,
        input_side_factors.reshape(rows, left), output_factors.reshape(rows, right),
        query_order,
    ).T


def plain_shards(activations, out_grads, input_side_factors, output_factors, query_order):
    rank = input_side_factors.shape[1]
    all_v = lax.all_gather(input_side_factors, "tok", axis=0, tiled=True)
    all_u = lax.all_gather(output_factors, "tok", axis=0, tiled=True)
    sides = []
    for tokens, factors in ((activations, all_v), (out_grads, all_u)):
        matrix = factors.reshape(-1, factors.shape[2])
        partial = lax.dot_general(tokens, matrix, NT, preferred_element_type=jnp.float32)
        sides.append(lax.psum_scatter(partial, "feat", scatter_dimension=0, tiled=True))
    product = (sides[0] * sides[1]).reshape(sides[0].shape[0], -1, rank)
    return jnp.take(jnp.sum(product, axis=2) * rank ** (-0.5), query_order, axis=1)


def solution(mesh):
    n = mesh.shape["tok"]
    small = 2 <= n <= 4 and mesh.shape["grp"] == 2 and mesh.shape["feat"] == 4
    return jax.shard_map(
        functools.partial(fused_shards, n) if small else plain_shards,
        mesh=mesh,
        in_specs=(
            P(("grp", "tok"), "feat"),
            P(("grp", "tok"), "feat"),
            P("tok", None, "feat"),
            P("tok", None, "feat"),
            P(),
        ),
        out_specs=P(("grp", "tok", "feat"), None),
        check_vma=False,
    )
```

```python
import functools

import jax
import jax.numpy as jnp
from jax import lax
from jax.experimental import pallas as pl
from jax.experimental.pallas import tpu as pltpu
from jax.sharding import PartitionSpec as P

MESH = pl.DeviceIdType.MESH
NT = (((1,), (1,)), ((), ()))
PIECES = 3


def segments(left_half, right_half):
    width = (left_half + right_half) // PIECES
    result = []
    for j in range(PIECES):
        lo, hi = j * width, (j + 1) * width
        segs = []
        if lo < left_half:
            segs.append((False, lo, 0, min(hi, left_half) - lo))
        if hi > left_half:
            start = max(lo, left_half)
            segs.append((True, start - left_half, start - lo, hi - start))
        result.append(segs)
    return width, result


def fused(n, rank, a_hbm, g_hbm, v_hbm, u_hbm, order_ref, out_ref,
          a, g, w, part, core_in, pair, pair_in,
          load_a, load_w, z_send, z_recv, y_send, y_recv,
          c_send, c_recv, x_send, x_recv, e_send, e_recv):
    y, z, f = lax.axis_index("grp"), lax.axis_index("tok"), lax.axis_index("feat")
    c, x = lax.rem(f, 2), lax.div(f, 2)
    left_half, right_half = a.shape[1] // 2, g.shape[1] // 2
    width, segs = segments(left_half, right_half)
    rows, last = w.shape[3], PIECES - 1
    chunk = out_ref.shape[1]
    core_mate, x_mate = 2 * x + (1 - c), 2 * (1 - x) + c

    barrier = pltpu.get_barrier_semaphore()
    pl.semaphore_signal(barrier, inc=1, device_id={"grp": 1 - y}, device_id_type=MESH)
    pl.semaphore_signal(barrier, inc=1, device_id={"feat": core_mate}, device_id_type=MESH)
    pl.semaphore_signal(barrier, inc=1, device_id={"feat": x_mate}, device_id_type=MESH)

    @pl.when(z > 0)
    def _():
        pl.semaphore_signal(barrier, inc=1, device_id={"tok": z - 1}, device_id_type=MESH)

    @pl.when(z < n - 1)
    def _():
        pl.semaphore_signal(barrier, inc=1, device_id={"tok": z + 1}, device_id_type=MESH)

    def own_loads(which, h, j):
        made = []
        for i, (is_right, off, at, wide) in enumerate(segs[j]):
            src = u_hbm if is_right else v_hbm
            half = right_half if is_right else left_half
            made.append(pltpu.make_async_copy(
                src.at[:, pl.ds(pl.multiple_of(h * half + off, 128), wide)],
                w.at[z, h, j, :, pl.ds(at, wide)],
                load_w.at[which, j, i]))
        return made

    for which, h in ((0, y), (1, 1 - y)):
        for j in range(PIECES):
            for copy in own_loads(which, h, j):
                copy.start()
    copy_a = pltpu.make_async_copy(a_hbm, a, load_a.at[0])
    copy_g = pltpu.make_async_copy(g_hbm, g, load_a.at[1])
    copy_a.start()
    copy_g.start()

    peers = 3 + jnp.where(z > 0, 1, 0) + jnp.where(z < n - 1, 1, 0)
    pl.semaphore_wait(barrier, peers)

    def source(way, d):
        return z - d if way == 0 else z + d

    def arrives(way, d):
        return z >= d if way == 0 else z < n - d

    def has_next(way):
        return z < n - 1 if way == 0 else z > 0

    def z_copy(way, d, j, s):
        return pltpu.make_async_remote_copy(
            src_ref=w.at[s, y, j], dst_ref=w.at[s, y, j],
            send_sem=z_send.at[way, d - 1, j], recv_sem=z_recv.at[way, d - 1, j],
            device_id={"tok": z + 1 if way == 0 else z - 1}, device_id_type=MESH)

    def from_end(way, d):
        return z == d if way == 0 else z == n - 1 - d

    def extra_copy(way, d, s):
        return pltpu.make_async_remote_copy(
            src_ref=w.at[s, 1 - y, last], dst_ref=w.at[s, 1 - y, last],
            send_sem=e_send.at[way, d - 1], recv_sem=e_recv.at[way, d - 1],
            device_id={"tok": z + 1 if way == 0 else z - 1}, device_id_type=MESH)

    def unless_extra(way, d, j, action):
        if j == last:
            pl.when(jnp.logical_not(from_end(way, d)))(action)
        else:
            action()

    def y_copy(way, d, j, h):
        s = source(way, d)
        return pltpu.make_async_remote_copy(
            src_ref=w.at[s, h, j], dst_ref=w.at[s, h, j],
            send_sem=y_send.at[way, d - 1, j], recv_sem=y_recv.at[way, d - 1, j],
            device_id={"grp": 1 - y}, device_id_type=MESH)

    def core_copy(b):
        return pltpu.make_async_remote_copy(
            src_ref=part.at[b, 1 - c], dst_ref=core_in.at[b],
            send_sem=c_send.at[b], recv_sem=c_recv.at[b],
            device_id={"feat": core_mate}, device_id_type=MESH)

    def x_copy(b):
        return pltpu.make_async_remote_copy(
            src_ref=pair.at[b], dst_ref=pair_in.at[b],
            send_sem=x_send.at[b], recv_sem=x_recv.at[b],
            device_id={"feat": x_mate}, device_id_type=MESH)

    def add_piece(b, s, h, j, fresh):
        for is_right, off, at, wide in segs[j]:
            side = g if is_right else a
            half = right_half if is_right else left_half
            columns = pl.ds(pl.multiple_of(h * half + off, 128), wide)
            product = lax.dot_general(
                side[:, columns], w[s, h, j, :, pl.ds(at, wide)], NT,
                preferred_element_type=jnp.float32)
            for m in range(4):
                to = (b, m % 2, m // 2, slice(None), pl.ds(rows if is_right else 0, rows))
                some = product[m * chunk:(m + 1) * chunk]
                if fresh and off == 0:
                    part[to] = some
                else:
                    part[to] += some

    def across_x(b):
        core_copy(b).wait_recv()
        pair[b] = part[b, c, 1 - x] + core_in[b, 1 - x]
        x_copy(b).start()

    def finish(b, s):
        x_copy(b).wait_recv()
        total = part[b, c, x] + core_in[b, x] + pair_in[b]
        product = total[:, :rows] * total[:, rows:]
        query = s * (rows // rank) + lax.div(
            lax.broadcasted_iota(jnp.int32, (out_ref.shape[0], rows), 1), rank)
        column = lax.broadcasted_iota(jnp.int32, query.shape, 0)
        wanted = jnp.zeros_like(query)
        for k in range(out_ref.shape[0]):
            wanted = jnp.where(column == k, order_ref[k], wanted)
        pick = jnp.where(query == wanted, 1.0, 0.0).astype(jnp.float32)
        out_ref[...] += lax.dot_general(
            pick, product, NT, precision=lax.Precision.HIGHEST,
            preferred_element_type=jnp.float32) * (rank ** -0.5)

    def block(way, d):
        return 1 + 2 * (d - 1) + way

    out_ref[...] = jnp.zeros_like(out_ref)
    for j in range(PIECES):
        for copy in own_loads(0, y, j):
            copy.wait()
        for way in (0, 1):
            @pl.when(has_next(way))
            def _():
                z_copy(way, 1, j, z).start()
    for j in range(PIECES):
        for copy in own_loads(1, 1 - y, j):
            copy.wait()
    for way in (0, 1):
        @pl.when(from_end(way, 0))
        def _():
            extra_copy(way, 1, z).start()

    def each_way(d, action):
        for way in (0, 1):
            @pl.when(arrives(way, d))
            def _():
                action(way)

    slots = [(d, j) for d in range(1, n) for j in range(PIECES)]

    def other_half(d, j):
        def action(way):
            unless_extra(way, d, j, lambda: y_copy(way, d, j, 1 - y).wait_recv())
            add_piece(block(way, d), source(way, d), 1 - y, j, False)
            if j == PIECES - 1:
                core_copy(block(way, d)).start()
        each_way(d, action)

    for k, (d, j) in enumerate(slots):
        def pass_on(way):
            s = source(way, d)
            z_copy(way, d, j, s).wait_recv()
            if d < n - 1:
                @pl.when(has_next(way))
                def _():
                    z_copy(way, d + 1, j, s).start()
            unless_extra(way, d, j, lambda: y_copy(way, d, j, y).start())
        each_way(d, pass_on)
        if d == 1:
            if j == 0:
                copy_a.wait()
                copy_g.wait()
            add_piece(0, z, 0, j, True)
            add_piece(0, z, 1, j, False)
            if j == PIECES - 1:
                core_copy(0).start()
        each_way(d, lambda way: add_piece(block(way, d), source(way, d), y, j, True))
        if k >= 1:
            other_half(*slots[k - 1])
        if j == last:
            for way in (0, 1):
                @pl.when(from_end(way, d))
                def _():
                    extra_copy(way, d, source(way, d)).wait_recv()
                    if d < n - 1:
                        extra_copy(way, d + 1, source(way, d)).start()
        if j == min(1, PIECES - 1):
            if d == 2:
                across_x(0)
            if d >= 2:
                each_way(d - 1, lambda way: across_x(block(way, d - 1)))
        if j == PIECES - 1:
            if d == 2:
                finish(0, z)
            if d >= 3:
                each_way(d - 2, lambda way: finish(block(way, d - 2), source(way, d - 2)))
    other_half(*slots[-1])
    each_way(n - 1, lambda way: across_x(block(way, n - 1)))
    for d in range(max(n - 2, 1), n):
        each_way(d, lambda way: finish(block(way, d), source(way, d)))

    for way in (0, 1):
        for d in range(1, n):
            @pl.when(from_end(way, d - 1))
            def _():
                extra_copy(way, d, source(way, d - 1)).wait_send()

            sends = (arrives(way, d - 1) if d > 1 else z >= 0) & has_next(way)

            @pl.when(sends)
            def _():
                for j in range(PIECES):
                    z_copy(way, d, j, source(way, d - 1)).wait_send()

            @pl.when(arrives(way, d))
            def _():
                for j in range(PIECES):
                    unless_extra(way, d, j, lambda: y_copy(way, d, j, y).wait_send())
                core_copy(block(way, d)).wait_send()
                x_copy(block(way, d)).wait_send()
    core_copy(0).wait_send()
    x_copy(0).wait_send()


def fused_shards(n, activations, out_grads, input_side_factors, output_factors, query_order):
    per_block, rank, left = input_side_factors.shape
    right = output_factors.shape[2]
    rows = per_block * rank
    tokens = activations.shape[0]
    chunk = tokens // 4
    total = query_order.shape[0]
    width, segs = segments(left // 2, right // 2)
    most = max(len(s) for s in segs)
    blocks = 2 * n - 1
    dma = pltpu.SemaphoreType.DMA
    f32 = jnp.float32
    return pl.pallas_call(
        functools.partial(fused, n, rank),
        out_shape=jax.ShapeDtypeStruct((total, chunk), f32),
        in_specs=[pl.BlockSpec(memory_space=pl.ANY)] * 4 + [pl.BlockSpec(memory_space=pltpu.SMEM)],
        out_specs=pl.BlockSpec(memory_space=pltpu.VMEM),
        scratch_shapes=[
            pltpu.VMEM((tokens, left), activations.dtype),
            pltpu.VMEM((tokens, right), out_grads.dtype),
            pltpu.VMEM((n, 2, PIECES, rows, width), input_side_factors.dtype),
            pltpu.VMEM((blocks, 2, 2, chunk, 2 * rows), f32),
            pltpu.VMEM((blocks, 2, chunk, 2 * rows), f32),
            pltpu.VMEM((blocks, chunk, 2 * rows), f32),
            pltpu.VMEM((blocks, chunk, 2 * rows), f32),
            dma((2,)),
            dma((2, PIECES, most)),
            dma((2, n - 1, PIECES)),
            dma((2, n - 1, PIECES)),
            dma((2, n - 1, PIECES)),
            dma((2, n - 1, PIECES)),
            dma((blocks,)),
            dma((blocks,)),
            dma((blocks,)),
            dma((blocks,)),
            dma((2, n - 1)),
            dma((2, n - 1)),
        ],
        compiler_params=pltpu.CompilerParams(
            collective_id=0, has_side_effects=True, vmem_limit_bytes=60 * 2**20),
        cost_estimate=pl.CostEstimate(
            flops=2 * tokens * n * rows * (left + right),
            bytes_accessed=2 * (tokens + rows) * (left + right), transcendentals=0),
    )(
        activations, out_grads,
        input_side_factors.reshape(rows, left), output_factors.reshape(rows, right),
        query_order,
    ).T


def plain_shards(activations, out_grads, input_side_factors, output_factors, query_order):
    rank = input_side_factors.shape[1]
    all_v = lax.all_gather(input_side_factors, "tok", axis=0, tiled=True)
    all_u = lax.all_gather(output_factors, "tok", axis=0, tiled=True)
    sides = []
    for tokens, factors in ((activations, all_v), (out_grads, all_u)):
        matrix = factors.reshape(-1, factors.shape[2])
        partial = lax.dot_general(tokens, matrix, NT, preferred_element_type=jnp.float32)
        sides.append(lax.psum_scatter(partial, "feat", scatter_dimension=0, tiled=True))
    product = (sides[0] * sides[1]).reshape(sides[0].shape[0], -1, rank)
    return jnp.take(jnp.sum(product, axis=2) * rank ** (-0.5), query_order, axis=1)


def solution(mesh):
    n = mesh.shape["tok"]
    small = 2 <= n <= 4 and mesh.shape["grp"] == 2 and mesh.shape["feat"] == 4
    return jax.shard_map(
        functools.partial(fused_shards, n) if small else plain_shards,
        mesh=mesh,
        in_specs=(
            P(("grp", "tok"), "feat"),
            P(("grp", "tok"), "feat"),
            P("tok", None, "feat"),
            P("tok", None, "feat"),
            P(),
        ),
        out_specs=P(("grp", "tok", "feat"), None),
        check_vma=False,
    )
```
